32 devices in a mesh: group: 2 (over x), vocab: 8 (over z, y), dp: 2 (over core).
Axes of the slice: x: 2, y: 2, z: 4, core: 2. Of those that a mesh axis runs over, the one named last changes fastest.
Arguments:
- hidden_rows: bfloat16 [256, 4096], P(('vocab', 'dp')), may hold values from -96 to 96
- lm_head: bfloat16 [4096, 20480], P(None, ('vocab', 'dp')), may hold values from -1 to 1
- draft_len: int32 [128], P(('group', 'vocab', 'dp')), parts along dimension 0, may hold values from 1 to 3, as said below
- draft_tokens: int32 [64, 3], P(('vocab', 'dp')), may hold values from 0 to 20479
- draft_prob: float32 [64, 3], P(('vocab', 'dp')), may hold values from 0.05 to 1
- accept_uniform: float32 [128, 3], P(('group', 'vocab', 'dp')), parts along dimension 0, may hold values from 0 to 1
Outputs:
- accept_ratio: float32 [128, 3], P(('group', 'vocab', 'dp')), parts along dimension 0
- accepted: int32 [128], P(('group', 'vocab', 'dp')), parts along dimension 0
- correction: float32 [128, 20480], P(('group', 'vocab', 'dp')), parts along dimension 0
The draws below stay inside these ranges and needn't reach their ends.
There are 2 independent parts, one for each index of `group`. The reference program is written for one: setup_inputs(seed, part) draws one part's arguments, and reference() takes and returns one part's arrays. A program takes and returns all parts, laid end to end along the dimension named above; an argument that names none is the same for every part. Nothing has to cross between parts.
Inputs may be any that keep to these rules, and one draw needn't show every extreme that they name: In each aligned block of 4 requests (the requests of one device), draft_len sums to at most 8, and exactly that in at least one block of every draw.
All inputs are finite; a program needn't handle non-finite values.
Results may differ from the reference program's by a relative error of at most 0.0003.
Values may be sent and summed in bfloat16 or wider, within the bound.
A program may use at most 128 MiB of HBM per device.

```python
import math
import jax
import jax.numpy as jnp

D = 4096
DRAFT = 3
REQ_DEV = 4
SLOTS = 4
REQUESTS = 64
VOCAB = 20480


def head_parts(key, column_id):
    key = jax.random.fold_in(jax.random.fold_in(key, 11), column_id)
    scale_key, value_key = jax.random.split(key)
    spread = jnp.exp(jax.random.uniform(scale_key, (), jnp.float32, math.log(0.7), math.log(1.1)))
    values = jax.random.truncated_normal(value_key, -4.0, 4.0, (D,), jnp.float32)
    return (values, spread)


def head_column(key, column_id):
    values, spread = head_parts(key, column_id)
    return values * spread / math.sqrt(D)


def request_draws(key):
    key = jax.random.fold_in(key, 29)
    token_key, lift_key, top_key, low_key = jax.random.split(key, 4)
    entry_total = REQUESTS * DRAFT
    tokens = jax.random.randint(token_key, (entry_total,), 0, VOCAB)
    top_at = jax.random.randint(top_key, (), 0, entry_total)
    low_at = (top_at + 1 + jax.random.randint(low_key, (), 0, entry_total - 1)) % entry_total
    tokens = tokens.at[top_at].set(VOCAB - 1).at[low_at].set(0)
    lift = jax.random.uniform(lift_key, (REQUESTS, DRAFT), jnp.float32, -2.5, 2.0)
    return (tokens.reshape(REQUESTS, DRAFT).astype(jnp.int32), lift)


def draw_lm_head(key, part):
    columns = jax.vmap(lambda column_id: head_column(key, column_id))(jnp.arange(VOCAB, dtype=jnp.int32))
    return columns.T.astype(jnp.bfloat16)


def draw_draft_tokens(key, part):
    tokens, lift = request_draws(key)
    return tokens


def draw_draft_prob(key, part):
    tokens, lift = request_draws(key)
    key = jax.random.fold_in(key, 17)
    factor = jnp.exp(jax.random.uniform(key, (REQUESTS, DRAFT), jnp.float32, math.log(0.3), math.log(3.0)))
    return jnp.clip(jax.nn.sigmoid(lift) * factor, 0.05, 1.0)


def draw_hidden_rows(key, part):
    tokens, lift = request_draws(key)
    base_key = key
    key = jax.random.fold_in(key, 5)
    total_rows = REQUESTS * SLOTS
    scale_key, value_key = jax.random.split(key, 2)
    scales = jnp.exp(jax.random.uniform(scale_key, (total_rows, 1), jnp.float32, math.log(0.8), math.log(1.6)))
    values = jax.random.truncated_normal(value_key, -4.0, 4.0, (total_rows, D), jnp.float32) * scales
    spread_square = 0.797
    sigma_square = (scales[:, 0] * scales[:, 0] * spread_square).reshape(REQUESTS, SLOTS)[:, :DRAFT]
    target = math.log(VOCAB) + 0.5 * sigma_square + lift
    column_values, column_spread = jax.vmap(lambda column_id: head_parts(base_key, column_id))(tokens.reshape(-1))
    lifted = target.reshape(-1)[:, None] * column_values / (column_spread[:, None] * math.sqrt(D))
    values = values.reshape(REQUESTS, SLOTS, D)
    values = values.at[:, :DRAFT, :].add(lifted.reshape(REQUESTS, DRAFT, D))
    values = values.reshape(total_rows, D)
    return jnp.clip(values, -96.0, 96.0).astype(jnp.bfloat16)


def draw_draft_len(key, part):
    key = jax.random.fold_in(key, 7)
    level_key, heavy_key, first_key, second_key = jax.random.split(key, 4)
    device_total = REQUESTS // REQ_DEV
    pair_total = REQUESTS // 2
    device_ids = jnp.arange(device_total, dtype=jnp.int32)
    level = jnp.maximum(jax.random.randint(level_key, (device_total,), 0, 5) - 2, 0)
    heavy = jax.random.randint(heavy_key, (), 0, device_total)
    level = jnp.where(device_ids == heavy, 2, level)
    ceiling = jnp.repeat(2 + level, REQ_DEV // 2)
    first = jax.random.randint(first_key, (pair_total,), 1, jnp.minimum(3, ceiling - 1) + 1)
    second = jax.random.randint(second_key, (pair_total,), 1, ceiling - first + 1)
    filled = jnp.repeat(device_ids == heavy, REQ_DEV // 2)
    second = jnp.where(filled, ceiling - first, second)
    return jnp.stack([first, second], axis=1).reshape(REQUESTS).astype(jnp.int32)


def block_scale(own_key, dims, cuts, low, top_value):
    def one(axis_at, blocks):
        draws = jax.random.uniform(jax.random.fold_in(jax.random.fold_in(own_key, 6), axis_at), (blocks,), jnp.float32, low / len(cuts), top_value / len(cuts))
        return jnp.repeat(jnp.exp(draws), dims[axis_at] // blocks).reshape((-1,) + (1,) * (len(dims) - axis_at - 1))

    factor_of = one(*cuts[0])
    for cut in cuts[1:]:
        factor_of = factor_of * one(*cut)
    return factor_of


def setup_inputs(seed: int = 0, part: int = 0) -> dict:
    keys = jax.random.split(jax.random.key(seed), 7)
    part_splits = jax.random.split(jax.random.fold_in(keys[6], part), 7)
    return {
        "hidden_rows": draw_hidden_rows(jax.random.fold_in(keys[6], 71), part),
        "lm_head": draw_lm_head(jax.random.fold_in(keys[6], 71), part),
        "draft_len": draw_draft_len(jax.random.fold_in(jax.random.fold_in(keys[6], part), 71), part),
        "draft_tokens": draw_draft_tokens(jax.random.fold_in(keys[6], 71), part),
        "draft_prob": draw_draft_prob(jax.random.fold_in(keys[6], 71), part),
        "accept_uniform": jnp.clip(1.0 * jax.random.uniform(part_splits[5], (REQUESTS, DRAFT), jnp.float32) ** block_scale(part_splits[5], (REQUESTS, DRAFT), ((0, 16),), -0.2, 0.2), 0.0, 1.0),
    }


def reference(hidden_rows, lm_head, draft_len, draft_tokens, draft_prob, accept_uniform):
    logits = jnp.dot(hidden_rows, lm_head, preferred_element_type=jnp.float32)
    row_max = jnp.max(logits, axis=1)
    row_total = jnp.sum(jnp.exp(logits - row_max[:, None]), axis=1)
    request_ids = jnp.arange(REQUESTS, dtype=jnp.int32)
    slot_rows = request_ids[:, None] * SLOTS + jnp.arange(DRAFT, dtype=jnp.int32)[None, :]
    drafted = logits[slot_rows, draft_tokens]
    p_draft = jnp.exp(drafted - row_max[slot_rows]) / row_total[slot_rows]
    live_slot = jnp.arange(DRAFT, dtype=jnp.int32)[None, :] < draft_len[:, None]
    accept_ratio = jnp.where(live_slot, jnp.minimum(1.0, p_draft / draft_prob), 0.0)
    passed = (accept_uniform < accept_ratio).astype(jnp.int32)
    accepted = jnp.sum(jnp.cumprod(passed, axis=1), axis=1).astype(jnp.int32)
    rejected = accepted < draft_len
    pick_slot = jnp.minimum(accepted, DRAFT - 1)[:, None]
    drafted_token = jnp.take_along_axis(draft_tokens, pick_slot, axis=1)[:, 0]
    removed = jnp.where(rejected, jnp.take_along_axis(draft_prob, pick_slot, axis=1)[:, 0], 0.0)
    token_prob = jnp.take_along_axis(p_draft, pick_slot, axis=1)[:, 0]
    scale_back = 1.0 - jnp.minimum(token_prob, removed)
    chosen = request_ids * SLOTS + accepted
    target_prob = jnp.exp(logits[chosen] - row_max[chosen][:, None]) / row_total[chosen][:, None]
    is_drafted = jnp.arange(VOCAB, dtype=jnp.int32)[None, :] == drafted_token[:, None]
    residual = jnp.maximum(target_prob - jnp.where(is_drafted, removed[:, None], 0.0), 0.0)
    correction = VOCAB * residual / scale_back[:, None]
    return accept_ratio, accepted, correction
```

```python
import functools

import jax
import jax.numpy as jnp
from jax import lax
from jax.experimental import pallas as pl
from jax.experimental.pallas import tpu as pltpu
from jax.sharding import PartitionSpec as P

MESH = pl.DeviceIdType.MESH
CHUNKS = 4
CODE_TOP = 65535.0
CODE_STEPS = 2880.0
F32 = jnp.float32


def main_kernel(
    nv, nd,
    hid_ref, head_ref, len_ref, tok_ref, prob_ref, uni_ref,
    res_out, code_out,
    head_v, rows_v, meta_v, meta_send, acc_v, stat_v, res_v, words_v,
    head_sem, rows_recv, rows_send, meta_recv, meta_sent, stat_recv, stat_sent,
    res_recv, res_sent, code_recv, code_sent, local_sem,
):
    n = nv * nd
    total = 2 * n
    outer = nv // 2
    g = lax.axis_index("group")
    v = lax.axis_index("vocab")
    c = lax.axis_index("dp")
    h = g % 2
    base = g - h
    me = v * nd + c
    zz, yy = v // 2, v % 2
    flat = h * n + me
    half = hid_ref.shape[0] // 2
    slots = 4
    width = hid_ref.shape[1] // CHUNKS
    rows = n * half
    columns = head_ref.shape[1]

    def head_copy(k):
        at = pl.ds(k * width, width)
        return pltpu.make_async_copy(head_ref.at[at], head_v.at[at], head_sem.at[k])

    for k in range(CHUNKS):
        head_copy(k).start()

    def device_of(t):
        return (base + t // n, (t % n) // nd, t % nd)

    barrier = pltpu.get_barrier_semaphore()

    @pl.loop(1, total)
    def _(i):
        pl.semaphore_signal(barrier, inc=1, device_id=device_of((flat + i) % total), device_id_type=MESH)

    own = jnp.where(h == 0, hid_ref[0:half, :], hid_ref[half : 2 * half, :])
    for k in range(CHUNKS):
        rows_v[k * n + me] = own[:, k * width : (k + 1) * width]

    lane = lax.broadcasted_iota(jnp.int32, (half, 128), 1)
    sub = lax.broadcasted_iota(jnp.int32, (half, 128), 0)
    for part in range(2):
        block = jnp.zeros((half, 128), F32)
        for r in range(half // slots):
            req = part * (half // slots) + r
            mine = (sub // slots) == r
            block = jnp.where(mine & (lane == 3), len_ref[req].astype(F32), block)
            for s in range(slots - 1):
                at = sub == r * slots + s
                block = jnp.where(at & (lane == 0), tok_ref[req, s].astype(F32), block)
                block = jnp.where(at & (lane == 1), prob_ref[req, s], block)
                block = jnp.where(at & (lane == 2), uni_ref[req, s], block)
            at = sub == r * slots + slots - 1
            block = jnp.where(at & (lane == 0), -1.0, block)
            block = jnp.where(at & (lane == 1), 1.0, block)
        meta_send[part] = block
    meta_v[flat] = meta_send[h]

    pl.semaphore_wait(barrier, total - 1)

    def send_rows(k, src, device):
        at = k * n + src
        pltpu.make_async_remote_copy(
            rows_v.at[at], rows_v.at[at], rows_send, rows_recv.at[at], device_id=device, device_id_type=MESH
        ).start()

    def wait_rows(k, src):
        at = k * n + src
        pltpu.make_async_copy(rows_v.at[at], rows_v.at[at], rows_recv.at[at]).wait()

    for k in range(CHUNKS):
        @pl.loop(1, outer)
        def _(d):
            send_rows(k, me, (g, ((zz + d) % outer) * 2 + yy, c))

        send_rows(k, me, (g, zz * 2 + 1 - yy, c))
        send_rows(k, me, (g, v, 1 - c))

    @pl.loop(1, total)
    def _(i):
        t = (flat + i) % total
        pltpu.make_async_remote_copy(
            meta_send.at[t // n], meta_v.at[flat], meta_sent, meta_recv,
            device_id=device_of(t), device_id_type=MESH,
        ).start()

    def forward_column(k):
        @pl.loop(1, outer)
        def _(d):
            src = (((zz + d) % outer) * 2 + yy) * nd + c
            wait_rows(k, src)
            send_rows(k, src, (g, zz * 2 + 1 - yy, c))
            send_rows(k, src, (g, v, 1 - c))

    def forward_pair(k):
        @pl.loop(0, outer)
        def _(d):
            src = (((zz + d) % outer) * 2 + 1 - yy) * nd + c
            wait_rows(k, src)
            send_rows(k, src, (g, v, 1 - c))

    def multiply(k):
        @pl.loop(0, nv)
        def _(d):
            wait_rows(k, ((v + d) % nv) * nd + 1 - c)

        head_copy(k).wait()
        left = rows_v[k * n : (k + 1) * n].reshape(rows, width)

        @pl.loop(0, columns // 256)
        def _(j):
            at = pl.ds(pl.multiple_of(j * 256, 256), 256)
            product = jnp.dot(left, head_v[k * width : (k + 1) * width, at], preferred_element_type=F32)
            if k == 0:
                acc_v[:, at] = product
            else:
                acc_v[:, at] += product

    for t in range(CHUNKS + 2):
        if t < CHUNKS:
            forward_column(t)
        if 0 <= t - 1 < CHUNKS:
            forward_pair(t - 1)
        if 0 <= t - 2 < CHUNKS:
            multiply(t - 2)

    every = meta_v.at[pl.ds(0, total - 1)]
    pltpu.make_async_copy(every, every, meta_recv).wait()
    metas = [meta_v[q * n : (q + 1) * n].reshape(rows, 128) for q in range(2)]
    token, prob = metas[0][:, 0:1], metas[0][:, 1:2]

    logits = acc_v[...]
    local_max = jnp.max(logits, axis=1, keepdims=True)
    local_total = jnp.sum(jnp.exp(logits - local_max), axis=1, keepdims=True)
    column_ids = me * columns + lax.broadcasted_iota(jnp.int32, (rows, columns), 1)
    picked = jnp.sum(jnp.where(column_ids == token.astype(jnp.int32), logits, 0.0), axis=1, keepdims=True)
    wide_lane = lax.broadcasted_iota(jnp.int32, (rows, 128), 1)
    stats = jnp.where(wide_lane == 0, local_max, jnp.where(wide_lane == 1, local_total, picked))
    stat_v[me] = jnp.transpose(stats)[0:4, :]

    @pl.loop(1, n)
    def _(i):
        t = (me + i) % n
        pltpu.make_async_remote_copy(
            stat_v.at[me], stat_v.at[me], stat_sent, stat_recv,
            device_id=(g, t // nd, t % nd), device_id_type=MESH,
        ).start()

    every = stat_v.at[pl.ds(0, n - 1)]
    pltpu.make_async_copy(every, every, stat_recv).wait()
    all_stats = stat_v[...]
    all_max = all_stats[:, 0:1, :]
    top = jnp.max(all_max, axis=0)
    whole = jnp.sum(all_stats[:, 1:2, :] * jnp.exp(all_max - top[None]), axis=0)
    draft = jnp.sum(all_stats[:, 2:3, :], axis=0)
    tall = lax.broadcasted_iota(jnp.int32, (128, rows), 0)
    turned = jnp.transpose(jnp.where(tall == 0, top, jnp.where(tall == 1, whole, draft)))
    row_max, row_total, drafted = turned[:, 0:1], turned[:, 1:2], turned[:, 2:3]

    slot = lax.broadcasted_iota(jnp.int32, (rows, 1), 0) % slots
    is_draft = slot < slots - 1
    weight = jnp.where(is_draft, jnp.exp(drafted - row_max), 0.0)
    p_draft = weight / row_total
    bound = jnp.where(is_draft, jnp.minimum(1.0, 1.01 * (row_total - weight) + 1e-6), 1.0)
    origin = row_max + jnp.log(bound)
    code = jnp.clip(jnp.round((logits - origin) * CODE_STEPS) + CODE_TOP, 0.0, CODE_TOP)
    high = jnp.floor(code * (1.0 / 256.0))
    low = (code - high * 256.0).astype(jnp.bfloat16)
    high = high.astype(jnp.bfloat16)

    picks = []
    vocab_all = float(columns * n)
    requests = rows // slots
    owner = lax.broadcasted_iota(jnp.int32, (rows, requests), 0) // slots
    pick_at = lax.broadcasted_iota(jnp.int32, (rows, requests), 1)
    for q in range(2):
        uniform, length = metas[q][:, 2:3], metas[q][:, 3:4]
        live = slot.astype(F32) < length
        ratio = jnp.where(live, jnp.minimum(1.0, p_draft / prob), 0.0)
        passed = jnp.broadcast_to(jnp.where(uniform < ratio, 1.0, 0.0), (rows, 128))
        wide_slot = lax.broadcasted_iota(jnp.int32, (rows, 128), 0) % slots
        lead = passed
        for s in range(1, slots - 1):
            lead = lead * jnp.where(wide_slot >= s, pltpu.roll(passed, s, 0), 1.0)
        before = jnp.where(wide_slot == 0, 1.0, pltpu.roll(lead, 1, 0))
        chosen = before * (1.0 - lead)
        removed = jnp.where(live, prob, 0.0)
        scale = vocab_all / (1.0 - jnp.minimum(p_draft, removed))
        record = jnp.where(wide_lane == 3, slot.astype(F32), 0.0)
        record = jnp.where(wide_lane == 4, scale * bound / row_total, record)
        record = jnp.where(wide_lane == 5, scale * jnp.maximum(p_draft - removed, 0.0), record)
        record = jnp.where(wide_lane == 6, token + 1.0, record)
        record = jnp.where(chosen > 0.0, record, 0.0)
        record = jnp.where(wide_lane == wide_slot, jnp.where(wide_slot < slots - 1, ratio, record), record)
        res_v[q] = record.reshape(n, half, 128)
        picks.append(jnp.where(owner == pick_at, chosen[:, 0:1], 0.0))
    pick = jnp.concatenate(picks, axis=1).astype(jnp.bfloat16)

    to_partner = pltpu.make_async_remote_copy(
        res_v.at[1 - h, me], res_out.at[h], res_sent, res_recv,
        device_id=(base + 1 - h, v, c), device_id_type=MESH,
    )
    to_partner.start()
    to_self = pltpu.make_async_copy(res_v.at[h, me], res_out.at[h], local_sem.at[0])
    to_self.start()

    contract = (((0,), (0,)), ((), ()))
    sel_high = lax.dot_general(pick, high, contract, preferred_element_type=F32)
    sel_low = lax.dot_general(pick, low, contract, preferred_element_type=F32)
    sel = (sel_high * 256.0 + sel_low).astype(jnp.int32)
    words = sel[:, : columns // 2] | (sel[:, columns // 2 :] << 16)
    each = half // slots
    for i in range(total):
        words_v[i] = words[i * each : (i + 1) * each, :]

    @pl.loop(1, total)
    def _(i):
        t = (flat + i) % total
        pltpu.make_async_remote_copy(
            words_v.at[t], code_out.at[flat], code_sent, code_recv,
            device_id=device_of(t), device_id_type=MESH,
        ).start()

    own_words = pltpu.make_async_copy(words_v.at[flat], code_out.at[flat], local_sem.at[1])
    own_words.start()
    own_words.wait()
    to_self.wait()
    to_partner.wait()
    for ref, sem, count in (
        (rows_v, rows_send, CHUNKS * (n - 1)),
        (meta_v, meta_sent, total - 1),
        (stat_v, stat_sent, n - 1),
        (words_v, code_sent, total - 1),
        (code_out, code_recv, total - 1),
    ):
        every = ref.at[pl.ds(0, count)]
        pltpu.make_async_copy(every, every, sem).wait()


def decode_kernel(n, res_ref, code_ref, ratio_ref, accepted_ref, out_ref):
    half = res_ref.shape[1]
    slots = 4
    each = half // slots
    wide = code_ref.shape[2]
    records = []
    for h in range(2):
        for r in range(each):
            records.append(jnp.sum(res_ref[h, r * slots : (r + 1) * slots, :], axis=0, keepdims=True))
    for i, record in enumerate(records):
        accepted_ref[i] = record[0, 3].astype(jnp.int32)
    record = jnp.concatenate(records, axis=0)
    ratio_ref[...] = record[:, 0 : slots - 1]
    scale, at_token = record[:, 4:5], record[:, 5:6]
    token = record[:, 6:7].astype(jnp.int32) - 1
    ids = lax.broadcasted_iota(jnp.int32, (2 * each, wide), 1)

    @pl.loop(0, n)
    def _(i):
        word = jnp.concatenate([code_ref[i], code_ref[n + i]], axis=0)
        for part, code in enumerate((word & 65535, (word >> 16) & 65535)):
            start = pl.multiple_of((2 * i + part) * wide, 128)
            value = jnp.exp((code.astype(F32) - CODE_TOP) * (1.0 / CODE_STEPS)) * scale
            out_ref[:, pl.ds(start, wide)] = jnp.where(ids + start == token, at_token, value)


def body(hidden_rows, lm_head, draft_len, draft_tokens, draft_prob, accept_uniform):
    nv, nd = lax.axis_size("vocab"), lax.axis_size("dp")
    n = nv * nd
    half = hidden_rows.shape[0] // 2
    depth, columns = lm_head.shape
    width = depth // CHUNKS
    rows = n * half
    each = half // 4
    vmem = pl.BlockSpec(memory_space=pltpu.VMEM)
    smem = pl.BlockSpec(memory_space=pltpu.SMEM)
    dma = pltpu.SemaphoreType.DMA
    res, codes = pl.pallas_call(
        functools.partial(main_kernel, nv, nd),
        out_shape=(
            jax.ShapeDtypeStruct((2, half, 128), F32),
            jax.ShapeDtypeStruct((2 * n, each, columns // 2), jnp.int32),
        ),
        in_specs=[vmem, pl.BlockSpec(memory_space=pl.ANY), smem, smem, smem, smem],
        out_specs=(vmem, vmem),
        scratch_shapes=[
            pltpu.VMEM((depth, columns), jnp.bfloat16),
            pltpu.VMEM((CHUNKS * n, half, width), jnp.bfloat16),
            pltpu.VMEM((2 * n, half, 128), F32),
            pltpu.VMEM((2, half, 128), F32),
            pltpu.VMEM((rows, columns), F32),
            pltpu.VMEM((n, 4, rows), F32),
            pltpu.VMEM((2, n, half, 128), F32),
            pltpu.VMEM((2 * n, each, columns // 2), jnp.int32),
            dma((CHUNKS,)),
            dma((CHUNKS * n,)),
            dma, dma, dma, dma, dma, dma, dma, dma, dma,
            dma((2,)),
        ],
        compiler_params=pltpu.CompilerParams(
            collective_id=0, has_side_effects=True, vmem_limit_bytes=48 * 1024 * 1024
        ),
        name="verify",
    )(hidden_rows, lm_head, draft_len, draft_tokens, draft_prob, accept_uniform)
    return pl.pallas_call(
        functools.partial(decode_kernel, n),
        out_shape=(
            jax.ShapeDtypeStruct((2 * each, 3), F32),
            jax.ShapeDtypeStruct((2 * each,), jnp.int32),
            jax.ShapeDtypeStruct((2 * each, n * columns), F32),
        ),
        in_specs=[vmem, vmem],
        out_specs=(vmem, smem, vmem),
        name="decode",
    )(res, codes)


def solution(mesh):
    in_specs = (
        P(("vocab", "dp"), None),
        P(None, ("vocab", "dp")),
        P(("group", "vocab", "dp")),
        P(("vocab", "dp"), None),
        P(("vocab", "dp"), None),
        P(("group", "vocab", "dp"), None),
    )
    out_specs = (
        P(("group", "vocab", "dp"), None),
        P(("group", "vocab", "dp")),
        P(("group", "vocab", "dp"), None),
    )
    return jax.shard_map(body, mesh=mesh, in_specs=in_specs, out_specs=out_specs, check_vma=False)
```

```python
import functools

import jax
import jax.numpy as jnp
from jax import lax
from jax.experimental import pallas as pl
from jax.experimental.pallas import tpu as pltpu
from jax.sharding import PartitionSpec as P

MESH = pl.DeviceIdType.MESH
CHUNKS = 4
CODE_TOP = 65535.0
CODE_STEPS = 2880.0
F32 = jnp.float32


def main_kernel(
    nv, nd,
    hid_hbm, head_ref, len_hbm, tok_hbm, prob_hbm, uni_hbm,
    res_out, code_out,
    hid_ref, len_ref, tok_ref, prob_ref, uni_ref, head_v, rows_v, meta_v, meta_send, acc_v, stat_v, res_v, words_v,
    head_sem, rows_recv, rows_send, meta_recv, meta_sent, stat_recv, stat_sent,
    res_recv, res_sent, code_recv, code_sent, local_sem, small_sem,
):
    n = nv * nd
    total = 2 * n
    outer = nv // 2
    g = lax.axis_index("group")
    v = lax.axis_index("vocab")
    c = lax.axis_index("dp")
    h = g % 2
    base = g - h
    me = v * nd + c
    zz, yy = v // 2, v % 2
    flat = h * n + me
    half = hid_hbm.shape[0] // 2
    slots = 4
    width = hid_hbm.shape[1] // CHUNKS
    rows = n * half
    columns = head_ref.shape[1]

    def head_copy(k):
        at = pl.ds(k * width, width)
        return pltpu.make_async_copy(head_ref.at[at], head_v.at[at], head_sem.at[k])

    smalls = [
        pltpu.make_async_copy(src, dst, small_sem.at[i])
        for i, (src, dst) in enumerate((
            (hid_hbm, hid_ref), (len_hbm, len_ref), (tok_hbm, tok_ref), (prob_hbm, prob_ref), (uni_hbm, uni_ref),
        ))
    ]
    for copy in smalls:
        copy.start()
    for k in range(CHUNKS):
        head_copy(k).start()

    def device_of(t):
        return (base + t // n, (t % n) // nd, t % nd)

    barrier = pltpu.get_barrier_semaphore()

    @pl.loop(1, total)
    def _(i):
        pl.semaphore_signal(barrier, inc=1, device_id=device_of((flat + i) % total), device_id_type=MESH)

    smalls[0].wait()
    own = jnp.where(h == 0, hid_ref[0:half, :], hid_ref[half : 2 * half, :])
    for k in range(CHUNKS):
        rows_v[k * n + me] = own[:, k * width : (k + 1) * width]

    for copy in smalls[1:]:
        copy.wait()
    lane = lax.broadcasted_iota(jnp.int32, (half, 128), 1)
    sub = lax.broadcasted_iota(jnp.int32, (half, 128), 0)
    for part in range(2):
        block = jnp.zeros((half, 128), F32)
        for r in range(half // slots):
            req = part * (half // slots) + r
            mine = (sub // slots) == r
            block = jnp.where(mine & (lane == 3), len_ref[req].astype(F32), block)
            for s in range(slots - 1):
                at = sub == r * slots + s
                block = jnp.where(at & (lane == 0), tok_ref[req, s].astype(F32), block)
                block = jnp.where(at & (lane == 1), prob_ref[req, s], block)
                block = jnp.where(at & (lane == 2), uni_ref[req, s], block)
            at = sub == r * slots + slots - 1
            block = jnp.where(at & (lane == 0), -1.0, block)
            block = jnp.where(at & (lane == 1), 1.0, block)
        meta_send[part] = block
    meta_v[flat] = meta_send[h]

    pl.semaphore_wait(barrier, total - 1)

    def send_rows(k, src, device):
        at = k * n + src
        pltpu.make_async_remote_copy(
            rows_v.at[at], rows_v.at[at], rows_send, rows_recv.at[at], device_id=device, device_id_type=MESH
        ).start()

    def wait_rows(k, src):
        at = k * n + src
        pltpu.make_async_copy(rows_v.at[at], rows_v.at[at], rows_recv.at[at]).wait()

    for k in range(CHUNKS):
        @pl.loop(1, outer)
        def _(d):
            send_rows(k, me, (g, ((zz + d) % outer) * 2 + yy, c))

        send_rows(k, me, (g, zz * 2 + 1 - yy, c))
        send_rows(k, me, (g, v, 1 - c))

    @pl.loop(1, total)
    def _(i):
        t = (flat + i) % total
        pltpu.make_async_remote_copy(
            meta_send.at[t // n], meta_v.at[flat], meta_sent, meta_recv,
            device_id=device_of(t), device_id_type=MESH,
        ).start()

    def forward_column(k):
        @pl.loop(1, outer)
        def _(d):
            src = (((zz + d) % outer) * 2 + yy) * nd + c
            wait_rows(k, src)
            send_rows(k, src, (g, zz * 2 + 1 - yy, c))
            send_rows(k, src, (g, v, 1 - c))

    def forward_pair(k):
        @pl.loop(0, outer)
        def _(d):
            src = (((zz + d) % outer) * 2 + 1 - yy) * nd + c
            wait_rows(k, src)
            send_rows(k, src, (g, v, 1 - c))

    def multiply(k):
        @pl.loop(0, nv)
        def _(d):
            wait_rows(k, ((v + d) % nv) * nd + 1 - c)

        head_copy(k).wait()
        left = rows_v[k * n : (k + 1) * n].reshape(rows, width)

        @pl.loop(0, columns // 256)
        def _(j):
            at = pl.ds(pl.multiple_of(j * 256, 256), 256)
            product = jnp.dot(left, head_v[k * width : (k + 1) * width, at], preferred_element_type=F32)
            if k == 0:
                acc_v[:, at] = product
            else:
                acc_v[:, at] += product

    for t in range(CHUNKS + 2):
        if t < CHUNKS:
            forward_column(t)
        if 0 <= t - 1 < CHUNKS:
            forward_pair(t - 1)
        if 0 <= t - 2 < CHUNKS:
            multiply(t - 2)

    every = meta_v.at[pl.ds(0, total - 1)]
    pltpu.make_async_copy(every, every, meta_recv).wait()
    metas = [meta_v[q * n : (q + 1) * n].reshape(rows, 128) for q in range(2)]
    token, prob = metas[0][:, 0:1], metas[0][:, 1:2]

    logits = acc_v[...]
    local_max = jnp.max(logits, axis=1, keepdims=True)
    local_total = jnp.sum(jnp.exp(logits - local_max), axis=1, keepdims=True)
    column_ids = me * columns + lax.broadcasted_iota(jnp.int32, (rows, columns), 1)
    picked = jnp.sum(jnp.where(column_ids == token.astype(jnp.int32), logits, 0.0), axis=1, keepdims=True)
    wide_lane = lax.broadcasted_iota(jnp.int32, (rows, 128), 1)
    stats = jnp.where(wide_lane == 0, local_max, jnp.where(wide_lane == 1, local_total, picked))
    stat_v[me] = jnp.transpose(stats)[0:4, :]

    @pl.loop(1, n)
    def _(i):
        t = (me + i) % n
        pltpu.make_async_remote_copy(
            stat_v.at[me], stat_v.at[me], stat_sent, stat_recv,
            device_id=(g, t // nd, t % nd), device_id_type=MESH,
        ).start()

    every = stat_v.at[pl.ds(0, n - 1)]
    pltpu.make_async_copy(every, every, stat_recv).wait()
    all_stats = stat_v[...]
    all_max = all_stats[:, 0:1, :]
    top = jnp.max(all_max, axis=0)
    whole = jnp.sum(all_stats[:, 1:2, :] * jnp.exp(all_max - top[None]), axis=0)
    draft = jnp.sum(all_stats[:, 2:3, :], axis=0)
    tall = lax.broadcasted_iota(jnp.int32, (128, rows), 0)
    turned = jnp.transpose(jnp.where(tall == 0, top, jnp.where(tall == 1, whole, draft)))
    row_max, row_total, drafted = turned[:, 0:1], turned[:, 1:2], turned[:, 2:3]

    slot = lax.broadcasted_iota(jnp.int32, (rows, 1), 0) % slots
    is_draft = slot < slots - 1
    weight = jnp.where(is_draft, jnp.exp(drafted - row_max), 0.0)
    p_draft = weight / row_total
    bound = jnp.where(is_draft, jnp.minimum(1.0, 1.01 * (row_total - weight) + 1e-6), 1.0)
    origin = row_max + jnp.log(bound)
    code = jnp.clip(jnp.round((logits - origin) * CODE_STEPS) + CODE_TOP, 0.0, CODE_TOP)
    high = jnp.floor(code * (1.0 / 256.0))
    low = (code - high * 256.0).astype(jnp.bfloat16)
    high = high.astype(jnp.bfloat16)

    picks = []
    vocab_all = float(columns * n)
    requests = rows // slots
    owner = lax.broadcasted_iota(jnp.int32, (rows, requests), 0) // slots
    pick_at = lax.broadcasted_iota(jnp.int32, (rows, requests), 1)
    for q in range(2):
        uniform, length = metas[q][:, 2:3], metas[q][:, 3:4]
        live = slot.astype(F32) < length
        ratio = jnp.where(live, jnp.minimum(1.0, p_draft / prob), 0.0)
        passed = jnp.broadcast_to(jnp.where(uniform < ratio, 1.0, 0.0), (rows, 128))
        wide_slot = lax.broadcasted_iota(jnp.int32, (rows, 128), 0) % slots
        lead = passed
        for s in range(1, slots - 1):
            lead = lead * jnp.where(wide_slot >= s, pltpu.roll(passed, s, 0), 1.0)
        before = jnp.where(wide_slot == 0, 1.0, pltpu.roll(lead, 1, 0))
        chosen = before * (1.0 - lead)
        removed = jnp.where(live, prob, 0.0)
        scale = vocab_all / (1.0 - jnp.minimum(p_draft, removed))
        record = jnp.where(wide_lane == 3, slot.astype(F32), 0.0)
        record = jnp.where(wide_lane == 4, scale * bound / row_total, record)
        record = jnp.where(wide_lane == 5, scale * jnp.maximum(p_draft - removed, 0.0), record)
        record = jnp.where(wide_lane == 6, token + 1.0, record)
        record = jnp.where(chosen > 0.0, record, 0.0)
        record = jnp.where(wide_lane == wide_slot, jnp.where(wide_slot < slots - 1, ratio, record), record)
        res_v[q] = record.reshape(n, half, 128)
        picks.append(jnp.where(owner == pick_at, chosen[:, 0:1], 0.0))
    pick = jnp.concatenate(picks, axis=1).astype(jnp.bfloat16)

    to_partner = pltpu.make_async_remote_copy(
        res_v.at[1 - h, me], res_out.at[h], res_sent, res_recv,
        device_id=(base + 1 - h, v, c), device_id_type=MESH,
    )
    to_partner.start()
    to_self = pltpu.make_async_copy(res_v.at[h, me], res_out.at[h], local_sem.at[0])
    to_self.start()

    contract = (((0,), (0,)), ((), ()))
    sel_high = lax.dot_general(pick, high, contract, preferred_element_type=F32)
    sel_low = lax.dot_general(pick, low, contract, preferred_element_type=F32)
    sel = (sel_high * 256.0 + sel_low).astype(jnp.int32)
    words = sel[:, : columns // 2] | (sel[:, columns // 2 :] << 16)
    each = half // slots
    for i in range(total):
        words_v[i] = words[i * each : (i + 1) * each, :]

    @pl.loop(1, total)
    def _(i):
        t = (flat + i) % total
        pltpu.make_async_remote_copy(
            words_v.at[t], code_out.at[flat], code_sent, code_recv,
            device_id=device_of(t), device_id_type=MESH,
        ).start()

    own_words = pltpu.make_async_copy(words_v.at[flat], code_out.at[flat], local_sem.at[1])
    own_words.start()
    own_words.wait()
    to_self.wait()
    to_partner.wait()
    for ref, sem, count in (
        (rows_v, rows_send, CHUNKS * (n - 1)),
        (meta_v, meta_sent, total - 1),
        (stat_v, stat_sent, n - 1),
        (words_v, code_sent, total - 1),
        (code_out, code_recv, total - 1),
    ):
        every = ref.at[pl.ds(0, count)]
        pltpu.make_async_copy(every, every, sem).wait()


def decode_kernel(n, res_ref, code_ref, ratio_ref, accepted_ref, out_ref):
    half = res_ref.shape[1]
    slots = 4
    each = half // slots
    wide = code_ref.shape[2]
    records = []
    for h in range(2):
        for r in range(each):
            records.append(jnp.sum(res_ref[h, r * slots : (r + 1) * slots, :], axis=0, keepdims=True))
    for i, record in enumerate(records):
        accepted_ref[i] = record[0, 3].astype(jnp.int32)
    record = jnp.concatenate(records, axis=0)
    ratio_ref[...] = record[:, 0 : slots - 1]
    scale, at_token = record[:, 4:5], record[:, 5:6]
    token = record[:, 6:7].astype(jnp.int32) - 1
    ids = lax.broadcasted_iota(jnp.int32, (2 * each, wide), 1)

    @pl.loop(0, n)
    def _(i):
        word = jnp.concatenate([code_ref[i], code_ref[n + i]], axis=0)
        for part, code in enumerate((word & 65535, (word >> 16) & 65535)):
            start = pl.multiple_of((2 * i + part) * wide, 128)
            value = jnp.exp((code.astype(F32) - CODE_TOP) * (1.0 / CODE_STEPS)) * scale
            out_ref[:, pl.ds(start, wide)] = jnp.where(ids + start == token, at_token, value)


def body(hidden_rows, lm_head, draft_len, draft_tokens, draft_prob, accept_uniform):
    nv, nd = lax.axis_size("vocab"), lax.axis_size("dp")
    n = nv * nd
    half = hidden_rows.shape[0] // 2
    depth, columns = lm_head.shape
    width = depth // CHUNKS
    rows = n * half
    each = half // 4
    vmem = pl.BlockSpec(memory_space=pltpu.VMEM)
    hbm = pl.BlockSpec(memory_space=pltpu.HBM)
    smem = pl.BlockSpec(memory_space=pltpu.SMEM)
    dma = pltpu.SemaphoreType.DMA
    res, codes = pl.pallas_call(
        functools.partial(main_kernel, nv, nd),
        out_shape=(
            jax.ShapeDtypeStruct((2, half, 128), F32),
            jax.ShapeDtypeStruct((2 * n, each, columns // 2), jnp.int32),
        ),
        in_specs=[hbm] * 6,
        out_specs=(hbm, hbm),
        scratch_shapes=[
            pltpu.VMEM(hidden_rows.shape, hidden_rows.dtype),
            pltpu.SMEM(draft_len.shape, draft_len.dtype),
            pltpu.SMEM(draft_tokens.shape, draft_tokens.dtype),
            pltpu.SMEM(draft_prob.shape, draft_prob.dtype),
            pltpu.SMEM(accept_uniform.shape, accept_uniform.dtype),
            pltpu.VMEM((depth, columns), jnp.bfloat16),
            pltpu.VMEM((CHUNKS * n, half, width), jnp.bfloat16),
            pltpu.VMEM((2 * n, half, 128), F32),
            pltpu.VMEM((2, half, 128), F32),
            pltpu.VMEM((rows, columns), F32),
            pltpu.VMEM((n, 4, rows), F32),
            pltpu.VMEM((2, n, half, 128), F32),
            pltpu.VMEM((2 * n, each, columns // 2), jnp.int32),
            dma((CHUNKS,)),
            dma((CHUNKS * n,)),
            dma, dma, dma, dma, dma, dma, dma, dma, dma,
            dma((2,)),
            dma((5,)),
        ],
        compiler_params=pltpu.CompilerParams(
            collective_id=0, has_side_effects=True, vmem_limit_bytes=63 * 1024 * 1024
        ),
        name="verify",
    )(hidden_rows, lm_head, draft_len, draft_tokens, draft_prob, accept_uniform)
    return pl.pallas_call(
        functools.partial(decode_kernel, n),
        out_shape=(
            jax.ShapeDtypeStruct((2 * each, 3), F32),
            jax.ShapeDtypeStruct((2 * each,), jnp.int32),
            jax.ShapeDtypeStruct((2 * each, n * columns), F32),
        ),
        in_specs=[vmem, vmem],
        out_specs=(vmem, smem, vmem),
        compiler_params=pltpu.CompilerParams(vmem_limit_bytes=63 * 1024 * 1024),
        name="decode",
    )(res, codes)


def solution(mesh):
    in_specs = (
        P(("vocab", "dp"), None),
        P(None, ("vocab", "dp")),
        P(("group", "vocab", "dp")),
        P(("vocab", "dp"), None),
        P(("vocab", "dp"), None),
        P(("group", "vocab", "dp"), None),
    )
    out_specs = (
        P(("group", "vocab", "dp"), None),
        P(("group", "vocab", "dp")),
        P(("group", "vocab", "dp"), None),
    )
    return jax.shard_map(body, mesh=mesh, in_specs=in_specs, out_specs=out_specs, check_vma=False)
```

```python
import functools

import jax
import jax.numpy as jnp
from jax import lax
from jax.experimental import pallas as pl
from jax.experimental.pallas import tpu as pltpu
from jax.sharding import PartitionSpec as P

MESH = pl.DeviceIdType.MESH
CHUNKS = 4
FIELDS = 128
CODE_TOP = 65535.0
CODE_STEPS = 2880.0
F32 = jnp.float32


def main_kernel(
    nv, nd,
    hid_hbm, head_ref, len_hbm, tok_hbm, prob_hbm, uni_hbm,
    res_out, code_out,
    hid_ref, len_ref, tok_ref, prob_ref, uni_ref, head_v, rows_a, rows_b, meta_in, meta_send, acc_v, stat_v, res_v, words_v,
    head_sem, rows_recv, rows_send, pair_recv, core_recv, meta_recv, meta_sent, stat_recv, stat_sent,
    res_recv, res_sent, code_recv, code_sent, local_sem, small_sem,
):
    n = nv * nd
    total = 2 * n
    outer = nv // 2
    g = lax.axis_index("group")
    v = lax.axis_index("vocab")
    c = lax.axis_index("dp")
    h = g % 2
    base = g - h
    me = v * nd + c
    zz, yy = v // 2, v % 2
    flat = h * n + me
    spot = (yy * nd + c) * outer + zz
    half = hid_hbm.shape[0] // 2
    slots = 4
    width = hid_hbm.shape[1] // CHUNKS
    rows = n * half
    columns = head_ref.shape[1]

    def head_copy(k):
        at = pl.ds(k * width, width)
        return pltpu.make_async_copy(head_ref.at[at], head_v.at[at], head_sem.at[k])

    smalls = [
        pltpu.make_async_copy(src, dst, small_sem.at[i])
        for i, (src, dst) in enumerate((
            (hid_hbm, hid_ref), (len_hbm, len_ref), (tok_hbm, tok_ref), (prob_hbm, prob_ref), (uni_hbm, uni_ref),
        ))
    ]
    for copy in smalls:
        copy.start()
    for k in range(CHUNKS):
        head_copy(k).start()

    def plane_peers(visit, planes):
        def around(tz, first):
            for py in range(2):
                ty = yy if py == 0 else 1 - yy
                for pc in range(2):
                    tc = c if pc == 0 else 1 - c
                    for ph in range(planes):
                        th = h if ph == 0 else 1 - h
                        if not (first and py == pc == ph == 0):
                            visit((base + th, tz * 2 + ty, tc), th, (ty * nd + tc) * outer + tz)

        around(zz, True)

        @pl.loop(1, outer)
        def _(d):
            tz = zz + d
            around(jnp.where(tz >= outer, tz - outer, tz), False)

    barrier = pltpu.get_barrier_semaphore()

    def greet(device, plane, place):
        pl.semaphore_signal(barrier, inc=1, device_id=device, device_id_type=MESH)

    plane_peers(greet, 2)

    smalls[0].wait()
    own = jnp.where(h == 0, hid_ref[0:half, :], hid_ref[half : 2 * half, :])
    def rows_of(k):
        return rows_b if k == CHUNKS - 1 else rows_a.at[k]

    for k in range(CHUNKS):
        rows_of(k)[spot, :, 0:width] = own[:, k * width : (k + 1) * width]

    for copy in smalls[1:]:
        copy.wait()
    lane = lax.broadcasted_iota(jnp.int32, (half, 128), 1)
    sub = lax.broadcasted_iota(jnp.int32, (half, 128), 0)
    for part in range(2):
        block = jnp.zeros((half, 128), F32)
        for r in range(half // slots):
            req = part * (half // slots) + r
            mine = (sub // slots) == r
            block = jnp.where(mine & (lane == 3), len_ref[req].astype(F32), block)
            for s in range(slots - 1):
                at = sub == r * slots + s
                block = jnp.where(at & (lane == 0), tok_ref[req, s].astype(F32), block)
                block = jnp.where(at & (lane == 1), prob_ref[req, s], block)
                block = jnp.where(at & (lane == 2), uni_ref[req, s], block)
            at = sub == r * slots + slots - 1
            block = jnp.where(at & (lane == 0), -1.0, block)
            block = jnp.where(at & (lane == 1), 1.0, block)
        meta_send[part] = block
    pl.semaphore_wait(barrier, total - 1)

    meta_swap = pltpu.make_async_remote_copy(
        meta_send.at[1 - h], meta_in, meta_sent, meta_recv,
        device_id=(base + 1 - h, v, c), device_id_type=MESH,
    )
    meta_swap.start()

    def send_column(k):
        @pl.loop(1, outer)
        def _(d):
            tz = zz + d
            tz = jnp.where(tz >= outer, tz - outer, tz)
            pltpu.make_async_remote_copy(
                rows_of(k).at[spot], rows_of(k).at[spot], rows_send.at[k], rows_recv.at[k],
                device_id=(g, tz * 2 + yy, c), device_id_type=MESH,
            ).start()

    def send_four(k, y, recv, device):
        at = pl.ds((y * nd + c) * outer, outer)
        pltpu.make_async_remote_copy(
            rows_of(k).at[at], rows_of(k).at[at], rows_send.at[k], recv, device_id=device, device_id_type=MESH
        ).start()

    def wait_blocks(k, count, sem):
        some = rows_of(k).at[pl.ds(0, count)]
        pltpu.make_async_copy(some, some, sem).wait()

    for k in range(CHUNKS - 1):
        send_column(k)
    meta_swap.wait()
    own_part, other_part = meta_send[h], meta_in[...]
    parts = [jnp.where(h == 0, own_part, other_part), jnp.where(h == 0, other_part, own_part)]
    fields = jnp.where(lane < 4, parts[0], jnp.where(lane < 6, pltpu.roll(parts[1], 2, 1), 0.0))
    piece = fields.astype(jnp.bfloat16).astype(F32)
    left_over = fields - piece
    second = left_over.astype(jnp.bfloat16).astype(F32)
    pieces = piece + pltpu.roll(second, 8, 1) + pltpu.roll(left_over - second, 16, 1)
    rows_b[spot, :, width : width + FIELDS] = pieces.astype(jnp.bfloat16)
    send_column(CHUNKS - 1)

    def forward_column(k):
        wait_blocks(k, outer - 1, rows_recv.at[k])
        send_four(k, yy, pair_recv.at[k], (g, zz * 2 + 1 - yy, c))
        send_four(k, yy, core_recv.at[2 * k], (g, v, 1 - c))

    def forward_pair(k):
        wait_blocks(k, outer, pair_recv.at[k])
        send_four(k, 1 - yy, core_recv.at[2 * k + 1], (g, v, 1 - c))

    def multiply(k):
        wait_blocks(k, outer, core_recv.at[2 * k])
        wait_blocks(k, outer, core_recv.at[2 * k + 1])
        head_copy(k).wait()
        left = rows_of(k)[:, :, 0:width].reshape(rows, width)

        @pl.loop(0, columns // 256)
        def _(j):
            at = pl.ds(pl.multiple_of(j * 256, 256), 256)
            product = jnp.dot(left, head_v[k * width : (k + 1) * width, at], preferred_element_type=F32)
            if k == 0:
                acc_v[:, at] = product
            else:
                acc_v[:, at] += product

    for t in range(CHUNKS + 2):
        if t < CHUNKS:
            forward_column(t)
        if 0 <= t - 1 < CHUNKS:
            forward_pair(t - 1)
        if 0 <= t - 2 < CHUNKS:
            multiply(t - 2)

    numbers = rows_b[:, :, width : width + FIELDS].reshape(rows, FIELDS).astype(F32)
    numbers = numbers + pltpu.roll(numbers, FIELDS - 8, 1) + pltpu.roll(numbers, FIELDS - 16, 1)
    token, prob = numbers[:, 0:1], numbers[:, 1:2]

    logits = acc_v[...]
    local_max = jnp.max(logits, axis=1, keepdims=True)
    local_total = jnp.sum(jnp.exp(logits - local_max), axis=1, keepdims=True)
    column_ids = me * columns + lax.broadcasted_iota(jnp.int32, (rows, columns), 1)
    picked = jnp.sum(jnp.where(column_ids == token.astype(jnp.int32), logits, 0.0), axis=1, keepdims=True)
    wide_lane = lax.broadcasted_iota(jnp.int32, (rows, 128), 1)
    stats = jnp.where(wide_lane == 0, local_max, jnp.where(wide_lane == 1, local_total, picked))
    stat_v[me] = jnp.transpose(stats)[0:4, :]

    def send_stats(device, plane, place):
        pltpu.make_async_remote_copy(
            stat_v.at[me], stat_v.at[me], stat_sent, stat_recv, device_id=device, device_id_type=MESH
        ).start()

    plane_peers(send_stats, 1)

    every = stat_v.at[pl.ds(0, n - 1)]
    pltpu.make_async_copy(every, every, stat_recv).wait()
    all_stats = stat_v[...]
    all_max = all_stats[:, 0:1, :]
    top = jnp.max(all_max, axis=0)
    whole = jnp.sum(all_stats[:, 1:2, :] * jnp.exp(all_max - top[None]), axis=0)
    draft = jnp.sum(all_stats[:, 2:3, :], axis=0)
    tall = lax.broadcasted_iota(jnp.int32, (128, rows), 0)
    turned = jnp.transpose(jnp.where(tall == 0, top, jnp.where(tall == 1, whole, draft)))
    row_max, row_total, drafted = turned[:, 0:1], turned[:, 1:2], turned[:, 2:3]

    slot = lax.broadcasted_iota(jnp.int32, (rows, 1), 0) % slots
    is_draft = slot < slots - 1
    weight = jnp.where(is_draft, jnp.exp(drafted - row_max), 0.0)
    p_draft = weight / row_total
    bound = jnp.where(is_draft, jnp.minimum(1.0, 1.01 * (row_total - weight) + 1e-6), 1.0)
    origin = row_max + jnp.log(bound)
    code = jnp.clip(jnp.round((logits - origin) * CODE_STEPS) + CODE_TOP, 0.0, CODE_TOP)
    high = jnp.floor(code * (1.0 / 256.0))
    low = (code - high * 256.0).astype(jnp.bfloat16)
    high = high.astype(jnp.bfloat16)

    picks = []
    vocab_all = float(columns * n)
    requests = rows // slots
    owner = lax.broadcasted_iota(jnp.int32, (rows, requests), 0) // slots
    pick_at = lax.broadcasted_iota(jnp.int32, (rows, requests), 1)
    for q in range(2):
        uniform, length = numbers[:, 2 + 2 * q : 3 + 2 * q], numbers[:, 3 + 2 * q : 4 + 2 * q]
        live = slot.astype(F32) < length
        ratio = jnp.where(live, jnp.minimum(1.0, p_draft / prob), 0.0)
        passed = jnp.broadcast_to(jnp.where(uniform < ratio, 1.0, 0.0), (rows, 128))
        wide_slot = lax.broadcasted_iota(jnp.int32, (rows, 128), 0) % slots
        lead = passed
        for s in range(1, slots - 1):
            lead = lead * jnp.where(wide_slot >= s, pltpu.roll(passed, s, 0), 1.0)
        before = jnp.where(wide_slot == 0, 1.0, pltpu.roll(lead, 1, 0))
        chosen = before * (1.0 - lead)
        removed = jnp.where(live, prob, 0.0)
        scale = vocab_all / (1.0 - jnp.minimum(p_draft, removed))
        record = jnp.where(wide_lane == 3, slot.astype(F32), 0.0)
        record = jnp.where(wide_lane == 4, scale * bound / row_total, record)
        record = jnp.where(wide_lane == 5, scale * jnp.maximum(p_draft - removed, 0.0), record)
        record = jnp.where(wide_lane == 6, token + 1.0, record)
        record = jnp.where(chosen > 0.0, record, 0.0)
        record = jnp.where(wide_lane == wide_slot, jnp.where(wide_slot < slots - 1, ratio, record), record)
        res_v[q] = record.reshape(n, half, 128)
        picks.append(jnp.where(owner == pick_at, chosen[:, 0:1], 0.0))
    pick = jnp.concatenate(picks, axis=1).astype(jnp.bfloat16)

    to_partner = pltpu.make_async_remote_copy(
        res_v.at[1 - h, spot], res_out.at[h], res_sent, res_recv,
        device_id=(base + 1 - h, v, c), device_id_type=MESH,
    )
    to_partner.start()
    to_self = pltpu.make_async_copy(res_v.at[h, spot], res_out.at[h], local_sem.at[0])
    to_self.start()

    contract = (((0,), (0,)), ((), ()))
    sel_high = lax.dot_general(pick, high, contract, preferred_element_type=F32)
    sel_low = lax.dot_general(pick, low, contract, preferred_element_type=F32)
    sel = (sel_high * 256.0 + sel_low).astype(jnp.int32)
    words = sel[:, : columns // 2] | (sel[:, columns // 2 :] << 16)
    each = half // slots
    for i in range(total):
        words_v[i] = words[i * each : (i + 1) * each, :]

    def send_words(device, plane, place):
        pltpu.make_async_remote_copy(
            words_v.at[plane * n + place], code_out.at[flat], code_sent, code_recv,
            device_id=device, device_id_type=MESH,
        ).start()

    plane_peers(send_words, 2)

    own_words = pltpu.make_async_copy(words_v.at[h * n + spot], code_out.at[flat], local_sem.at[1])
    own_words.start()
    own_words.wait()
    to_self.wait()
    to_partner.wait()
    for k in range(CHUNKS):
        wait_blocks(k, n - 1, rows_send.at[k])
    for ref, sem, count in (
        (stat_v, stat_sent, n - 1),
        (words_v, code_sent, total - 1),
        (code_out, code_recv, total - 1),
    ):
        every = ref.at[pl.ds(0, count)]
        pltpu.make_async_copy(every, every, sem).wait()


def decode_kernel(n, res_ref, code_ref, ratio_ref, accepted_ref, out_ref):
    half = res_ref.shape[1]
    slots = 4
    each = half // slots
    wide = code_ref.shape[2]
    records = []
    for h in range(2):
        for r in range(each):
            records.append(jnp.sum(res_ref[h, r * slots : (r + 1) * slots, :], axis=0, keepdims=True))
    for i, record in enumerate(records):
        accepted_ref[i] = record[0, 3].astype(jnp.int32)
    record = jnp.concatenate(records, axis=0)
    ratio_ref[...] = record[:, 0 : slots - 1]
    scale, at_token = record[:, 4:5], record[:, 5:6]
    token = record[:, 6:7].astype(jnp.int32) - 1
    ids = lax.broadcasted_iota(jnp.int32, (2 * each, wide), 1)

    @pl.loop(0, n)
    def _(i):
        word = jnp.concatenate([code_ref[i], code_ref[n + i]], axis=0)
        for part, code in enumerate((word & 65535, (word >> 16) & 65535)):
            start = pl.multiple_of((2 * i + part) * wide, 128)
            value = jnp.exp((code.astype(F32) - CODE_TOP) * (1.0 / CODE_STEPS)) * scale
            out_ref[:, pl.ds(start, wide)] = jnp.where(ids + start == token, at_token, value)


def body(hidden_rows, lm_head, draft_len, draft_tokens, draft_prob, accept_uniform):
    nv, nd = lax.axis_size("vocab"), lax.axis_size("dp")
    n = nv * nd
    half = hidden_rows.shape[0] // 2
    depth, columns = lm_head.shape
    width = depth // CHUNKS
    rows = n * half
    each = half // 4
    vmem = pl.BlockSpec(memory_space=pltpu.VMEM)
    hbm = pl.BlockSpec(memory_space=pltpu.HBM)
    smem = pl.BlockSpec(memory_space=pltpu.SMEM)
    dma = pltpu.SemaphoreType.DMA
    res, codes = pl.pallas_call(
        functools.partial(main_kernel, nv, nd),
        out_shape=(
            jax.ShapeDtypeStruct((2, half, 128), F32),
            jax.ShapeDtypeStruct((2 * n, each, columns // 2), jnp.int32),
        ),
        in_specs=[hbm] * 6,
        out_specs=(hbm, hbm),
        scratch_shapes=[
            pltpu.VMEM(hidden_rows.shape, hidden_rows.dtype),
            pltpu.SMEM(draft_len.shape, draft_len.dtype),
            pltpu.SMEM(draft_tokens.shape, draft_tokens.dtype),
            pltpu.SMEM(draft_prob.shape, draft_prob.dtype),
            pltpu.SMEM(accept_uniform.shape, accept_uniform.dtype),
            pltpu.VMEM((depth, columns), jnp.bfloat16),
            pltpu.VMEM((CHUNKS - 1, n, half, width), jnp.bfloat16),
            pltpu.VMEM((n, half, width + FIELDS), jnp.bfloat16),
            pltpu.VMEM((half, 128), F32),
            pltpu.VMEM((2, half, 128), F32),
            pltpu.VMEM((rows, columns), F32),
            pltpu.VMEM((n, 4, rows), F32),
            pltpu.VMEM((2, n, half, 128), F32),
            pltpu.VMEM((2 * n, each, columns // 2), jnp.int32),
            dma((CHUNKS,)),
            dma((CHUNKS,)),
            dma((CHUNKS,)),
            dma((CHUNKS,)),
            dma((2 * CHUNKS,)),
            dma, dma, dma, dma, dma, dma, dma, dma,
            dma((2,)),
            dma((5,)),
        ],
        compiler_params=pltpu.CompilerParams(
            collective_id=0, has_side_effects=True, vmem_limit_bytes=63 * 1024 * 1024
        ),
        name="verify",
    )(hidden_rows, lm_head, draft_len, draft_tokens, draft_prob, accept_uniform)
    return pl.pallas_call(
        functools.partial(decode_kernel, n),
        out_shape=(
            jax.ShapeDtypeStruct((2 * each, 3), F32),
            jax.ShapeDtypeStruct((2 * each,), jnp.int32),
            jax.ShapeDtypeStruct((2 * each, n * columns), F32),
        ),
        in_specs=[vmem, vmem],
        out_specs=(vmem, smem, vmem),
        compiler_params=pltpu.CompilerParams(vmem_limit_bytes=63 * 1024 * 1024),
        name="decode",
    )(res, codes)


def solution(mesh):
    in_specs = (
        P(("vocab", "dp"), None),
        P(None, ("vocab", "dp")),
        P(("group", "vocab", "dp")),
        P(("vocab", "dp"), None),
        P(("vocab", "dp"), None),
        P(("group", "vocab", "dp"), None),
    )
    out_specs = (
        P(("group", "vocab", "dp"), None),
        P(("group", "vocab", "dp")),
        P(("group", "vocab", "dp"), None),
    )
    return jax.shard_map(body, mesh=mesh, in_specs=in_specs, out_specs=out_specs, check_vma=False)
```

```python
import functools

import jax
import jax.numpy as jnp
from jax import lax
from jax.experimental import pallas as pl
from jax.experimental.pallas import tpu as pltpu
from jax.sharding import PartitionSpec as P

MESH = pl.DeviceIdType.MESH
CHUNKS = 4
FIELDS = 128
CODE_TOP = 65535.0
CODE_STEPS = 2880.0
F32 = jnp.float32


def main_kernel(
    nv, nd,
    hid_hbm, head_ref, len_hbm, tok_hbm, prob_hbm, uni_hbm,
    res_out, code_out,
    hid_ref, len_ref, tok_ref, prob_ref, uni_ref, head_v, rows_a, rows_b, meta_in, meta_send, acc_v, stat_v, res_v, words_v,
    head_sem, rows_recv, rows_send, pair_recv, core_recv, meta_recv, meta_sent, stat_recv, stat_sent,
    res_recv, res_sent, code_recv, code_sent, local_sem, small_sem,
):
    n = nv * nd
    total = 2 * n
    outer = nv // 2
    g = lax.axis_index("group")
    v = lax.axis_index("vocab")
    c = lax.axis_index("dp")
    h = g % 2
    base = g - h
    me = v * nd + c
    zz, yy = v // 2, v % 2
    flat = h * n + me
    spot = (yy * nd + c) * outer + zz
    half = hid_hbm.shape[0] // 2
    slots = 4
    width = hid_hbm.shape[1] // CHUNKS
    rows = n * half
    columns = head_ref.shape[1]

    def head_copy(k):
        at = pl.ds(k * width, width)
        return pltpu.make_async_copy(head_ref.at[at], head_v.at[at], head_sem.at[k])

    smalls = [
        pltpu.make_async_copy(src, dst, small_sem.at[i])
        for i, (src, dst) in enumerate((
            (hid_hbm, hid_ref), (len_hbm, len_ref), (tok_hbm, tok_ref), (prob_hbm, prob_ref), (uni_hbm, uni_ref),
        ))
    ]
    for copy in smalls:
        copy.start()
    for k in range(CHUNKS):
        head_copy(k).start()

    def plane_peers(visit, planes):
        def around(tz, first):
            for py in range(2):
                ty = yy if py == 0 else 1 - yy
                for pc in range(2):
                    tc = c if pc == 0 else 1 - c
                    for ph in range(planes):
                        th = h if ph == 0 else 1 - h
                        if not (first and py == pc == ph == 0):
                            visit((base + th, tz * 2 + ty, tc), th, (ty * nd + tc) * outer + tz)

        around(zz, True)

        @pl.loop(1, outer)
        def _(d):
            tz = zz + d
            around(jnp.where(tz >= outer, tz - outer, tz), False)

    barrier = pltpu.get_barrier_semaphore()

    def greet(device, plane, place):
        pl.semaphore_signal(barrier, inc=1, device_id=device, device_id_type=MESH)

    plane_peers(greet, 2)

    smalls[0].wait()
    own = jnp.where(h == 0, hid_ref[0:half, :], hid_ref[half : 2 * half, :])
    def rows_of(k):
        return rows_b if k == CHUNKS - 1 else rows_a.at[k]

    for k in range(CHUNKS):
        rows_of(k)[spot, :, 0:width] = own[:, k * width : (k + 1) * width]

    for copy in smalls[1:]:
        copy.wait()
    lane = lax.broadcasted_iota(jnp.int32, (half, 128), 1)
    sub = lax.broadcasted_iota(jnp.int32, (half, 128), 0)
    for part in range(2):
        block = jnp.zeros((half, 128), F32)
        for r in range(half // slots):
            req = part * (half // slots) + r
            mine = (sub // slots) == r
            block = jnp.where(mine & (lane == 3), len_ref[req].astype(F32), block)
            for s in range(slots - 1):
                at = sub == r * slots + s
                block = jnp.where(at & (lane == 0), tok_ref[req, s].astype(F32), block)
                block = jnp.where(at & (lane == 1), prob_ref[req, s], block)
                block = jnp.where(at & (lane == 2), uni_ref[req, s], block)
            at = sub == r * slots + slots - 1
            block = jnp.where(at & (lane == 0), -1.0, block)
            block = jnp.where(at & (lane == 1), 1.0, block)
        meta_send[part] = block
    pl.semaphore_wait(barrier, total - 1)

    meta_swap = pltpu.make_async_remote_copy(
        meta_send.at[1 - h], meta_in, meta_sent, meta_recv,
        device_id=(base + 1 - h, v, c), device_id_type=MESH,
    )
    meta_swap.start()

    def send_column(k):
        @pl.loop(1, outer)
        def _(d):
            tz = zz + d
            tz = jnp.where(tz >= outer, tz - outer, tz)
            pltpu.make_async_remote_copy(
                rows_of(k).at[spot], rows_of(k).at[spot], rows_send.at[k], rows_recv.at[k],
                device_id=(g, tz * 2 + yy, c), device_id_type=MESH,
            ).start()

    def send_four(k, y, recv, device):
        at = pl.ds((y * nd + c) * outer, outer)
        pltpu.make_async_remote_copy(
            rows_of(k).at[at], rows_of(k).at[at], rows_send.at[k], recv, device_id=device, device_id_type=MESH
        ).start()

    def wait_blocks(k, count, sem):
        some = rows_of(k).at[pl.ds(0, count)]
        pltpu.make_async_copy(some, some, sem).wait()

    for k in range(CHUNKS - 1):
        send_column(k)
    meta_swap.wait()
    own_part, other_part = meta_send[h], meta_in[...]
    parts = [jnp.where(h == 0, own_part, other_part), jnp.where(h == 0, other_part, own_part)]
    fields = jnp.where(lane < 4, parts[0], jnp.where(lane < 6, pltpu.roll(parts[1], 2, 1), 0.0))
    piece = fields.astype(jnp.bfloat16).astype(F32)
    left_over = fields - piece
    second = left_over.astype(jnp.bfloat16).astype(F32)
    pieces = piece + pltpu.roll(second, 8, 1) + pltpu.roll(left_over - second, 16, 1)
    rows_b[spot, :, width : width + FIELDS] = pieces.astype(jnp.bfloat16)
    send_column(CHUNKS - 1)

    def forward_column(k):
        wait_blocks(k, outer - 1, rows_recv.at[k])
        send_four(k, yy, pair_recv.at[k], (g, zz * 2 + 1 - yy, c))
        send_four(k, yy, core_recv.at[2 * k], (g, v, 1 - c))

    def forward_pair(k):
        wait_blocks(k, outer, pair_recv.at[k])
        send_four(k, 1 - yy, core_recv.at[2 * k + 1], (g, v, 1 - c))

    def multiply(k):
        wait_blocks(k, outer, core_recv.at[2 * k])
        wait_blocks(k, outer, core_recv.at[2 * k + 1])
        head_copy(k).wait()
        left = rows_of(k)[:, :, 0:width].reshape(rows, width)

        @pl.loop(0, columns // 256)
        def _(j):
            at = pl.ds(pl.multiple_of(j * 256, 256), 256)
            product = jnp.dot(left, head_v[k * width : (k + 1) * width, at], preferred_element_type=F32)
            if k == 0:
                acc_v[:, at] = product
            else:
                acc_v[:, at] += product

    for t in range(CHUNKS + 2):
        if t < CHUNKS:
            forward_column(t)
        if 0 <= t - 1 < CHUNKS:
            forward_pair(t - 1)
        if 0 <= t - 2 < CHUNKS:
            multiply(t - 2)

    numbers = rows_b[:, :, width : width + FIELDS].reshape(rows, FIELDS).astype(F32)
    numbers = numbers + pltpu.roll(numbers, FIELDS - 8, 1) + pltpu.roll(numbers, FIELDS - 16, 1)
    token, prob = numbers[:, 0:1], numbers[:, 1:2]

    logits = acc_v[...]
    local_max = jnp.max(logits, axis=1, keepdims=True)
    local_total = jnp.sum(jnp.exp(logits - local_max), axis=1, keepdims=True)
    column_ids = me * columns + lax.broadcasted_iota(jnp.int32, (rows, columns), 1)
    picked = jnp.sum(jnp.where(column_ids == token.astype(jnp.int32), logits, 0.0), axis=1, keepdims=True)
    wide_lane = lax.broadcasted_iota(jnp.int32, (rows, 128), 1)
    stats = jnp.where(wide_lane == 0, local_max, jnp.where(wide_lane == 1, local_total, picked))
    stat_v[me] = jnp.transpose(stats)[0:4, :]

    def send_stats(device, plane, place):
        pltpu.make_async_remote_copy(
            stat_v.at[me], stat_v.at[me], stat_sent, stat_recv, device_id=device, device_id_type=MESH
        ).start()

    plane_peers(send_stats, 1)

    every = stat_v.at[pl.ds(0, n - 1)]
    pltpu.make_async_copy(every, every, stat_recv).wait()
    all_stats = stat_v[...]
    all_max = all_stats[:, 0:1, :]
    top = jnp.max(all_max, axis=0)
    whole = jnp.sum(all_stats[:, 1:2, :] * jnp.exp(all_max - top[None]), axis=0)
    draft = jnp.sum(all_stats[:, 2:3, :], axis=0)
    tall = lax.broadcasted_iota(jnp.int32, (128, rows), 0)
    turned = jnp.transpose(jnp.where(tall == 0, top, jnp.where(tall == 1, whole, draft)))
    row_max, row_total, drafted = turned[:, 0:1], turned[:, 1:2], turned[:, 2:3]

    slot = lax.broadcasted_iota(jnp.int32, (rows, 1), 0) % slots
    is_draft = slot < slots - 1
    weight = jnp.where(is_draft, jnp.exp(drafted - row_max), 0.0)
    p_draft = weight / row_total
    bound = jnp.where(is_draft, jnp.minimum(1.0, 1.01 * (row_total - weight) + 1e-6), 1.0)
    origin = row_max + jnp.log(bound)
    code = jnp.clip(jnp.round((logits - origin) * CODE_STEPS) + CODE_TOP, 0.0, CODE_TOP)
    high = jnp.floor(code * (1.0 / 256.0))
    low = (code - high * 256.0).astype(jnp.bfloat16)
    high = high.astype(jnp.bfloat16)

    picks = []
    vocab_all = float(columns * n)
    requests = rows // slots
    owner = lax.broadcasted_iota(jnp.int32, (rows, requests), 0) // slots
    pick_at = lax.broadcasted_iota(jnp.int32, (rows, requests), 1)
    for q in range(2):
        uniform, length = numbers[:, 2 + 2 * q : 3 + 2 * q], numbers[:, 3 + 2 * q : 4 + 2 * q]
        live = slot.astype(F32) < length
        ratio = jnp.where(live, jnp.minimum(1.0, p_draft / prob), 0.0)
        passed = jnp.broadcast_to(jnp.where(uniform < ratio, 1.0, 0.0), (rows, 128))
        wide_slot = lax.broadcasted_iota(jnp.int32, (rows, 128), 0) % slots
        lead = passed
        for s in range(1, slots - 1):
            lead = lead * jnp.where(wide_slot >= s, pltpu.roll(passed, s, 0), 1.0)
        before = jnp.where(wide_slot == 0, 1.0, pltpu.roll(lead, 1, 0))
        chosen = before * (1.0 - lead)
        removed = jnp.where(live, prob, 0.0)
        scale = vocab_all / (1.0 - jnp.minimum(p_draft, removed))
        record = jnp.where(wide_lane == 3, slot.astype(F32), 0.0)
        record = jnp.where(wide_lane == 4, scale * bound / row_total, record)
        record = jnp.where(wide_lane == 5, scale * jnp.maximum(p_draft - removed, 0.0), record)
        record = jnp.where(wide_lane == 6, token + 1.0, record)
        record = jnp.where(chosen > 0.0, record, 0.0)
        record = jnp.where(wide_lane == wide_slot, jnp.where(wide_slot < slots - 1, ratio, record), record)
        res_v[q] = record.reshape(n, half, 128)
        picks.append(jnp.where(owner == pick_at, chosen[:, 0:1], 0.0))
    pick = jnp.concatenate(picks, axis=1).astype(jnp.bfloat16)

    to_partner = pltpu.make_async_remote_copy(
        res_v.at[1 - h, spot], res_out.at[h], res_sent, res_recv,
        device_id=(base + 1 - h, v, c), device_id_type=MESH,
    )
    to_partner.start()
    to_self = pltpu.make_async_copy(res_v.at[h, spot], res_out.at[h], local_sem.at[0])
    to_self.start()

    contract = (((0,), (0,)), ((), ()))
    sel_high = lax.dot_general(pick, high, contract, preferred_element_type=F32)
    sel_low = lax.dot_general(pick, low, contract, preferred_element_type=F32)
    sel = (sel_high * 256.0 + sel_low).astype(jnp.int32)
    words = sel[:, : columns // 2] | (sel[:, columns // 2 :] << 16)
    each = half // slots
    for i in range(total):
        words_v[i] = words[i * each : (i + 1) * each, :]

    def send_words(device, plane, place):
        pltpu.make_async_remote_copy(
            words_v.at[plane * n + place], code_out.at[flat], code_sent, code_recv,
            device_id=device, device_id_type=MESH,
        ).start()

    plane_peers(send_words, 2)

    own_words = pltpu.make_async_copy(words_v.at[h * n + spot], code_out.at[flat], local_sem.at[1])
    own_words.start()
    own_words.wait()
    to_self.wait()
    to_partner.wait()
    for k in range(CHUNKS):
        wait_blocks(k, n - 1, rows_send.at[k])
    for ref, sem, count in (
        (stat_v, stat_sent, n - 1),
        (words_v, code_sent, total - 1),
        (code_out, code_recv, total - 1),
    ):
        every = ref.at[pl.ds(0, count)]
        pltpu.make_async_copy(every, every, sem).wait()


def decode_kernel(n, res_ref, code_ref, ratio_ref, accepted_ref, out_ref):
    half = res_ref.shape[1]
    slots = 4
    each = half // slots
    wide = code_ref.shape[2]
    records = []
    for h in range(2):
        for r in range(each):
            records.append(jnp.sum(res_ref[h, r * slots : (r + 1) * slots, :], axis=0, keepdims=True))
    for i, record in enumerate(records):
        accepted_ref[i] = record[0, 3].astype(jnp.int32)
    record = jnp.concatenate(records, axis=0)
    ratio_ref[...] = record[:, 0 : slots - 1]
    scale, at_token = record[:, 4:5], record[:, 5:6]
    token = record[:, 6:7].astype(jnp.int32) - 1
    ids = lax.broadcasted_iota(jnp.int32, (2 * each, wide), 1)

    for i in range(n):
        word = jnp.concatenate([code_ref[i], code_ref[n + i]], axis=0)
        for part, code in enumerate((word & 65535, (word >> 16) & 65535)):
            start = (2 * i + part) * wide
            value = jnp.exp((code.astype(F32) - CODE_TOP) * (1.0 / CODE_STEPS)) * scale
            out_ref[:, start : start + wide] = jnp.where(ids + start == token, at_token, value)


def body(hidden_rows, lm_head, draft_len, draft_tokens, draft_prob, accept_uniform):
    nv, nd = lax.axis_size("vocab"), lax.axis_size("dp")
    n = nv * nd
    half = hidden_rows.shape[0] // 2
    depth, columns = lm_head.shape
    width = depth // CHUNKS
    rows = n * half
    each = half // 4
    vmem = pl.BlockSpec(memory_space=pltpu.VMEM)
    hbm = pl.BlockSpec(memory_space=pltpu.HBM)
    smem = pl.BlockSpec(memory_space=pltpu.SMEM)
    dma = pltpu.SemaphoreType.DMA
    res, codes = pl.pallas_call(
        functools.partial(main_kernel, nv, nd),
        out_shape=(
            jax.ShapeDtypeStruct((2, half, 128), F32),
            jax.ShapeDtypeStruct((2 * n, each, columns // 2), jnp.int32),
        ),
        in_specs=[hbm] * 6,
        out_specs=(hbm, hbm),
        scratch_shapes=[
            pltpu.VMEM(hidden_rows.shape, hidden_rows.dtype),
            pltpu.SMEM(draft_len.shape, draft_len.dtype),
            pltpu.SMEM(draft_tokens.shape, draft_tokens.dtype),
            pltpu.SMEM(draft_prob.shape, draft_prob.dtype),
            pltpu.SMEM(accept_uniform.shape, accept_uniform.dtype),
            pltpu.VMEM((depth, columns), jnp.bfloat16),
            pltpu.VMEM((CHUNKS - 1, n, half, width), jnp.bfloat16),
            pltpu.VMEM((n, half, width + FIELDS), jnp.bfloat16),
            pltpu.VMEM((half, 128), F32),
            pltpu.VMEM((2, half, 128), F32),
            pltpu.VMEM((rows, columns), F32),
            pltpu.VMEM((n, 4, rows), F32),
            pltpu.VMEM((2, n, half, 128), F32),
            pltpu.VMEM((2 * n, each, columns // 2), jnp.int32),
            dma((CHUNKS,)),
            dma((CHUNKS,)),
            dma((CHUNKS,)),
            dma((CHUNKS,)),
            dma((2 * CHUNKS,)),
            dma, dma, dma, dma, dma, dma, dma, dma,
            dma((2,)),
            dma((5,)),
        ],
        compiler_params=pltpu.CompilerParams(
            collective_id=0, has_side_effects=True, vmem_limit_bytes=63 * 1024 * 1024
        ),
        name="verify",
    )(hidden_rows, lm_head, draft_len, draft_tokens, draft_prob, accept_uniform)
    return pl.pallas_call(
        functools.partial(decode_kernel, n),
        out_shape=(
            jax.ShapeDtypeStruct((2 * each, 3), F32),
            jax.ShapeDtypeStruct((2 * each,), jnp.int32),
            jax.ShapeDtypeStruct((2 * each, n * columns), F32),
        ),
        in_specs=[vmem, vmem],
        out_specs=(vmem, smem, vmem),
        compiler_params=pltpu.CompilerParams(vmem_limit_bytes=63 * 1024 * 1024),
        name="decode",
    )(res, codes)


def solution(mesh):
    in_specs = (
        P(("vocab", "dp"), None),
        P(None, ("vocab", "dp")),
        P(("group", "vocab", "dp")),
        P(("vocab", "dp"), None),
        P(("vocab", "dp"), None),
        P(("group", "vocab", "dp"), None),
    )
    out_specs = (
        P(("group", "vocab", "dp"), None),
        P(("group", "vocab", "dp")),
        P(("group", "vocab", "dp"), None),
    )
    return jax.shard_map(body, mesh=mesh, in_specs=in_specs, out_specs=out_specs, check_vma=False)
```
